32 devices in a mesh: grp: 1, seq: 16 (over z, y, x), head: 1, srv: 2 (over core).
Axes of the slice: x: 2, y: 2, z: 4, core: 2. Of those that a mesh axis runs over, the one named last changes fastest.
Arguments:
- tokens: bfloat16 [4096, 4096], P(('grp', 'seq', 'srv'), 'head'), may hold values from -6 to 6
- norm_gain: float32 [4096], replicated, may hold values from 0.5 to 12, as said below
- wq: bfloat16 [4096, 4096], P(('seq', 'srv'), 'head'), may hold values from -0.09375 to 0.09375
- wk: bfloat16 [4096, 1024], P(('seq', 'srv'), 'head'), may hold values from -0.09375 to 0.09375
- wv: bfloat16 [4096, 1024], P(('seq', 'srv'), 'head'), may hold values from -0.09375 to 0.09375
- wo: bfloat16 [4096, 4096], P('head', ('seq', 'srv')), may hold values from -0.09375 to 0.09375
- doc_ids: int32 [4096], P(('grp', 'seq', 'srv')), may hold values from 0 to 7, never falling along the last dimension, each value on 1 to 3072 neighbouring positions
Outputs:
- mixed: bfloat16 [4096, 4096], P(('grp', 'seq', 'srv'), 'head')
The draws below stay inside these ranges and needn't reach their ends.
Inputs may be any that keep to these rules, and one draw needn't show every extreme that they name: `norm_gain`: the gain is positive.
All inputs are finite; a program needn't handle non-finite values.
Results may differ from the reference program's by a relative error of at most 0.015.
The reference program's roundings to bfloat16 on the way count: a program that leaves them out, or rounds other values in their place, can miss the bound.
Values may be sent and summed in bfloat16 or wider, within the bound.
A program may use at most 128 MiB of HBM per device.

```python
import math
import jax
import jax.numpy as jnp
import numpy as np
from jax import lax

MODEL_WIDTH = 4096
QUERY_HEADS = 32
KV_HEAD_COUNT = 8
HEAD_WIDTH = 128
DOCS = 8
SEQUENCE_TOKENS = 4096
DOC_MOST = 3072
N_HEAD = 1


def draw_norm_gain(key, part):
    low_end = 0.5
    high_end = 2.0
    unit = jax.random.uniform(key, (MODEL_WIDTH,), jnp.float32)
    return jnp.exp(jnp.log(low_end) + unit * (jnp.log(high_end) - jnp.log(low_end)))


def levels(rng, dims, split, low, top_value):
    def one(position, parts):
        draws = jax.random.uniform(jax.random.fold_in(jax.random.fold_in(rng, 6), position), (parts,), jnp.float32, low / len(split), top_value / len(split))
        return jnp.repeat(jnp.exp(draws), dims[position] // parts).reshape((-1,) + (1,) * (len(dims) - position - 1))

    loudness = one(*split[0])
    for cut in split[1:]:
        loudness = loudness * one(*cut)
    return loudness


def profile(count, total, most, skew):
    portions = [(1 << 20) // math.isqrt(standing ** skew) + 1 for standing in range(2, count + 1)]
    rest, given = total - most - (count - 1), [1] * (count - 1)
    while rest > 0:
        candidates = [i for i in range(count - 1) if given[i] < most]
        pool, remaining = sum([portions[i] for i in candidates]), rest
        for i in candidates:
            addition = min(most - given[i], max(1, remaining * portions[i] // pool), rest)
            given[i] = given[i] + addition
            rest = rest - addition
    return np.array([most] + given)


def ragged(stream_key, number_of, total, bound, skew):
    if number_of == 2:
        one = jax.random.randint(stream_key, (), max(1, total - bound), min(bound, total - 1) + 1)
        return jnp.stack([one, total - one])
    tallies = jnp.asarray(profile(number_of, total, bound, skew), jnp.int32)
    couples = (number_of - 1) // 2
    donor, sink = tallies[1:1 + 2 * couples:2], tallies[2:2 + 2 * couples:2]
    slack = jnp.minimum(donor - 1, bound - sink)
    shifted = jax.random.randint(jax.random.fold_in(stream_key, 1), (couples,), 0, 1 << 20) % (slack + 1)
    tallies = tallies.at[1:1 + 2 * couples:2].set(donor - shifted).at[2:2 + 2 * couples:2].set(sink + shifted)
    return tallies[jax.random.permutation(jax.random.fold_in(stream_key, 2), number_of)]


def scatter_about(key, shape, deviation, limit, shards=(), kind=jnp.bfloat16):
    factor_of = levels(key, shape, shards, -0.22, 0.18) if shards else 1.0
    array = jax.random.normal(key, shape, jnp.float32) * deviation * factor_of
    return jnp.minimum(jnp.maximum(array, -limit), limit).astype(kind)


def setup_inputs(seed: int = 0, part: int = 0) -> dict:
    splits = jax.random.split(jax.random.key(seed), 8)
    part_splits = jax.random.split(jax.random.fold_in(splits[7], part), 8)
    return {
        "tokens": scatter_about(part_splits[0], (SEQUENCE_TOKENS, MODEL_WIDTH), 1.0, 6.0, ((0, 32),)),
        "norm_gain": draw_norm_gain(jax.random.fold_in(splits[7], 71), part),
        "wq": scatter_about(splits[2], (MODEL_WIDTH, QUERY_HEADS * HEAD_WIDTH), MODEL_WIDTH ** -0.5, 0.09375, ((0, 32),)),
        "wk": scatter_about(splits[3], (MODEL_WIDTH, KV_HEAD_COUNT * HEAD_WIDTH), MODEL_WIDTH ** -0.5, 0.09375, ((0, 32),)),
        "wv": scatter_about(splits[4], (MODEL_WIDTH, KV_HEAD_COUNT * HEAD_WIDTH), MODEL_WIDTH ** -0.5, 0.09375, ((0, 32),)),
        "wo": scatter_about(splits[5], (QUERY_HEADS * HEAD_WIDTH, MODEL_WIDTH), (QUERY_HEADS * HEAD_WIDTH) ** -0.5, 0.09375, ((1, 32),)),
        "doc_ids": jnp.searchsorted(jnp.cumsum(ragged(part_splits[6], DOCS, SEQUENCE_TOKENS, DOC_MOST, 2)), jnp.arange(SEQUENCE_TOKENS), side="right").astype(jnp.int32),
    }


def rope(field, positions):
    half = field.shape[-1] // 2
    freqs = 500000.0 ** (-(jnp.arange(half, dtype=jnp.float32) * 2.0 / field.shape[-1]))
    angles = positions.astype(jnp.float32)[:, None] * freqs[None, :]
    cosine = jnp.cos(angles)[:, None, :]
    sine = jnp.sin(angles)[:, None, :]
    first = field[..., :half]
    second = field[..., half:]
    return jnp.concatenate([first * cosine - second * sine, second * cosine + first * sine], axis=-1)

def reference(tokens, norm_gain, wq, wk, wv, wo, doc_ids):
    source = tokens.astype(jnp.float32)
    mean_sq = lax.optimization_barrier(jnp.mean(source * source, axis=1, keepdims=True))
    normed_input = (source * lax.rsqrt(mean_sq + 1e-05) * norm_gain[None, :]).astype(jnp.bfloat16)
    positions = jnp.arange(SEQUENCE_TOKENS, dtype=jnp.int32)
    query_matrix = jnp.dot(normed_input, wq, preferred_element_type=jnp.float32).reshape(SEQUENCE_TOKENS, QUERY_HEADS, HEAD_WIDTH)
    query_matrix = rope(query_matrix, positions).astype(jnp.bfloat16)
    key_matrix = jnp.dot(normed_input, wk, preferred_element_type=jnp.float32).reshape(SEQUENCE_TOKENS, KV_HEAD_COUNT, HEAD_WIDTH)
    key_matrix = rope(key_matrix, positions).astype(jnp.bfloat16)
    value_matrix = jnp.dot(normed_input, wv, preferred_element_type=jnp.float32).reshape(SEQUENCE_TOKENS, KV_HEAD_COUNT, HEAD_WIDTH).astype(jnp.bfloat16)
    query_group = QUERY_HEADS // KV_HEAD_COUNT
    token_rows = 256
    scale = 1.0 / HEAD_WIDTH ** 0.5

    def one_block(block):
        start_index = (block * token_rows).astype(jnp.int32)
        rows_of_query = lax.dynamic_slice_in_dim(query_matrix, start_index, token_rows, 0).reshape(token_rows, KV_HEAD_COUNT, query_group, HEAD_WIDTH)
        query_pos = start_index + jnp.arange(token_rows, dtype=jnp.int32)
        query_doc = lax.dynamic_slice_in_dim(doc_ids, start_index, token_rows, 0)
        allowed = (positions[None, :] <= query_pos[:, None]) & (doc_ids[None, :] == query_doc[:, None])

        def single_head(head):
            key_head = jnp.take(key_matrix, head, axis=1).astype(jnp.float32)
            value_head = jnp.take(value_matrix, head, axis=1).astype(jnp.float32)
            query_head = jnp.take(rows_of_query, head, axis=1).astype(jnp.float32)
            scores = jnp.einsum('qgd,kd->qgk', query_head, key_head) * scale
            masked = jnp.where(allowed[:, None, :], scores, -1e+30)
            top = lax.optimization_barrier(jnp.max(masked, axis=2, keepdims=True))
            expd = jnp.where(allowed[:, None, :], jnp.exp(masked - top), 0.0)
            total = lax.optimization_barrier(jnp.sum(expd, axis=2, keepdims=True))
            weights = expd.astype(jnp.bfloat16).astype(jnp.float32)
            return jnp.einsum('qgk,kd->qgd', weights, value_head) / total
        head_list = lax.map(single_head, jnp.arange(KV_HEAD_COUNT, dtype=jnp.int32))
        return jnp.transpose(head_list, (1, 0, 2, 3)).reshape(token_rows, QUERY_HEADS * HEAD_WIDTH)
    attended = lax.map(one_block, jnp.arange(SEQUENCE_TOKENS // token_rows, dtype=jnp.int32))
    attended = attended.reshape(SEQUENCE_TOKENS, QUERY_HEADS * HEAD_WIDTH).astype(jnp.bfloat16)
    width = QUERY_HEADS * HEAD_WIDTH // N_HEAD
    summed = jnp.zeros((SEQUENCE_TOKENS, MODEL_WIDTH), jnp.float32)
    for shard in range(N_HEAD):
        part_term = jnp.dot(attended[:, shard * width:(shard + 1) * width], wo[shard * width:(shard + 1) * width, :], preferred_element_type=jnp.float32)
        summed = summed + part_term.astype(jnp.bfloat16).astype(jnp.float32)
    return (source + summed).astype(jnp.bfloat16)
```

```python
import functools
import math

import jax
import jax.numpy as jnp
from jax import lax
from jax.experimental import pallas as pl
from jax.experimental.pallas import tpu as pltpu
from jax.sharding import PartitionSpec as P

QUERY_HEADS = 32
KV_HEAD_COUNT = 8
HEAD_WIDTH = 128


def rope(field, positions):
    half = field.shape[-1] // 2
    freqs = 500000.0 ** (-(jnp.arange(half, dtype=jnp.float32) * 2.0 / field.shape[-1]))
    angles = positions.astype(jnp.float32)[:, None] * freqs[None, :]
    cosine = jnp.cos(angles)[:, None, :]
    sine = jnp.sin(angles)[:, None, :]
    first = field[..., :half]
    second = field[..., half:]
    return jnp.concatenate(
        [first * cosine - second * sine, second * cosine + first * sine], axis=-1
    )


def local(tokens, norm_gain, wq, wk, wv, wo, doc_ids):
    tok_rows = tokens.shape[0]
    head_size = HEAD_WIDTH
    kv_local = wk.shape[1] // head_size
    query_group = QUERY_HEADS // KV_HEAD_COUNT
    source = tokens.astype(jnp.float32)
    whole = lax.all_gather(tokens, "head", axis=1, tiled=True).astype(jnp.float32)
    mean_sq = jnp.mean(whole * whole, axis=1, keepdims=True)
    normed_input = (whole * lax.rsqrt(mean_sq + 1e-05) * norm_gain[None, :]).astype(jnp.bfloat16)
    query_acc = jnp.dot(
        normed_input,
        lax.all_gather(wq, ("seq", "srv"), axis=0, tiled=True),
        preferred_element_type=jnp.float32,
    )
    key_acc = jnp.dot(
        normed_input,
        lax.all_gather(wk, ("seq", "srv"), axis=0, tiled=True),
        preferred_element_type=jnp.float32,
    )
    value_acc = jnp.dot(
        normed_input,
        lax.all_gather(wv, ("seq", "srv"), axis=0, tiled=True),
        preferred_element_type=jnp.float32,
    )
    first_pos = lax.axis_index(("seq", "srv")) * tok_rows
    positions = first_pos + jnp.arange(tok_rows, dtype=jnp.int32)
    query_matrix = rope(query_acc.reshape(tok_rows, kv_local * query_group, head_size), positions)
    query_matrix = query_matrix.astype(jnp.bfloat16).reshape(
        tok_rows, kv_local, query_group, head_size
    )
    key_matrix = rope(key_acc.reshape(tok_rows, kv_local, head_size), positions).astype(
        jnp.bfloat16
    )
    key_matrix = key_matrix.reshape(tok_rows, kv_local * head_size)
    value_matrix = value_acc.astype(jnp.bfloat16)
    scale = 1.0 / head_size**0.5

    def attend_block(carry, key_rows, value_rows, doc_rows, key_pos):
        run_top, run_total, run_acc = carry
        key_heads = key_rows.reshape(key_rows.shape[0], kv_local, head_size)
        value_heads = value_rows.reshape(value_rows.shape[0], kv_local, head_size)
        scores = (
            jnp.einsum(
                "qcgd,kcd->qcgk", query_matrix, key_heads, preferred_element_type=jnp.float32
            )
            * scale
        )
        allowed = (
            (key_pos[None, :] <= positions[:, None])
            & (key_pos[None, :] >= 0)
            & (doc_rows[None, :] == doc_ids[:, None])
        )
        allowed = allowed[:, None, None, :]
        masked = jnp.where(allowed, scores, -1e30)
        new_top = jnp.maximum(run_top, jnp.max(masked, axis=3))
        expd = jnp.where(allowed, jnp.exp(masked - new_top[..., None]), 0.0)
        factor = jnp.exp(run_top - new_top)
        new_total = run_total * factor + jnp.sum(expd, axis=3)
        weights = expd.astype(jnp.bfloat16)
        update = jnp.einsum(
            "qcgk,kcd->qcgd", weights, value_heads, preferred_element_type=jnp.float32
        )
        return (new_top, new_total, run_acc * factor[..., None] + update)

    start_state = (
        jnp.full((tok_rows, kv_local, query_group), -1e30, jnp.float32),
        jnp.zeros((tok_rows, kv_local, query_group), jnp.float32),
        jnp.zeros((tok_rows, kv_local, query_group, head_size), jnp.float32),
    )
    key_piece = lax.all_gather(key_matrix, ("seq", "srv"), axis=0, tiled=True)
    value_piece = lax.all_gather(value_matrix, ("seq", "srv"), axis=0, tiled=True)
    doc_piece = lax.all_gather(doc_ids, ("seq", "srv"), axis=0, tiled=True)
    count = key_piece.shape[0]
    width = math.gcd(count, 512)

    def step(inner, index):
        offset = index * width
        key_rows = lax.dynamic_slice_in_dim(key_piece, offset, width, 0)
        value_rows = lax.dynamic_slice_in_dim(value_piece, offset, width, 0)
        doc_rows = lax.dynamic_slice_in_dim(doc_piece, offset, width, 0)
        key_pos = offset + jnp.arange(width, dtype=jnp.int32)
        return (attend_block(inner, key_rows, value_rows, doc_rows, key_pos), None)

    def run_all(inner):
        result, unused = lax.scan(step, inner, jnp.arange(count // width, dtype=jnp.int32))
        return result

    beyond = jnp.int32(0) > first_pos + tok_rows - 1
    before = doc_piece[count - 1] < doc_ids[0]
    final_top, final_total, final_acc = lax.cond(
        beyond | before, lambda inner: inner, run_all, start_state
    )
    attended = (final_acc / final_total[..., None]).astype(jnp.bfloat16)
    attended = attended.reshape(tok_rows, kv_local * query_group * head_size)
    terms = jnp.dot(
        attended,
        lax.all_gather(wo, ("seq", "srv"), axis=1, tiled=True),
        preferred_element_type=jnp.float32,
    )
    summed = lax.psum_scatter(
        terms.astype(jnp.bfloat16), "head", scatter_dimension=1, tiled=True
    ).astype(jnp.float32)
    return (source + summed).astype(jnp.bfloat16)


def attention_kernel(head_count, key_block, lo_ref, mid_ref, diag_ref, end_ref, first_ref,
                     q_ref, kv_ref, start_ref, out_ref, acc_ref, top_ref, total_ref):
    block = pl.program_id(0)
    rows = q_ref.shape[0]
    top_ref[...] = jnp.full_like(top_ref, -1e30)
    total_ref[...] = jnp.zeros_like(total_ref)
    acc_ref[...] = jnp.zeros_like(acc_ref)
    factor_log2 = 1.4426950408889634 / HEAD_WIDTH**0.5
    starts = start_ref[...]
    query_pos = (
        first_ref[0] + block * rows + lax.broadcasted_iota(jnp.int32, (rows, key_block), 0)
    )

    def visit(index, masked):
        offset = pl.multiple_of(index * key_block, key_block)
        keys = kv_ref[pl.ds(offset, key_block), :HEAD_WIDTH]
        values = kv_ref[pl.ds(offset, key_block), HEAD_WIDTH:]
        if masked:
            key_pos = offset + lax.broadcasted_iota(jnp.int32, (rows, key_block), 1)
            allowed = (key_pos <= query_pos) & (key_pos >= starts)
        for head in range(head_count):
            columns = slice(head * HEAD_WIDTH, (head + 1) * HEAD_WIDTH)
            scores = lax.dot_general(
                q_ref[:, columns], keys, (((1,), (1,)), ((), ())),
                preferred_element_type=jnp.float32,
            )
            if masked:
                scores = jnp.where(allowed, scores, -1e30)
            old_top = top_ref[head]
            new_top = jnp.maximum(old_top, jnp.max(scores, axis=1, keepdims=True))
            expd = jnp.exp2((scores - new_top[:, :1]) * factor_log2)
            factor = jnp.exp2((old_top - new_top) * factor_log2)
            top_ref[head] = new_top
            total_ref[head] = total_ref[head] * factor + jnp.sum(expd, axis=1, keepdims=True)
            acc_ref[:, columns] = acc_ref[:, columns] * factor + jnp.dot(
                expd.astype(jnp.bfloat16), values, preferred_element_type=jnp.float32
            )

    low, mid, diag, end = lo_ref[block], mid_ref[block], diag_ref[block], end_ref[block]

    @pl.loop(low, mid)
    def _(index):
        visit(index, True)

    @pl.loop(mid, diag)
    def _(index):
        visit(index, False)

    @pl.loop(diag, end)
    def _(index):
        visit(index, True)

    for head in range(head_count):
        columns = slice(head * HEAD_WIDTH, (head + 1) * HEAD_WIDTH)
        out_ref[:, columns] = (acc_ref[:, columns] / total_ref[head]).astype(jnp.bfloat16)


def attend(queries, keys_values, starts, first, query_block, key_block):
    tokens, width = queries.shape
    blocks = tokens // query_block
    head_count = width // HEAD_WIDTH
    begins = starts.reshape(blocks, query_block)
    query_first = first + jnp.arange(blocks, dtype=jnp.int32) * query_block
    low = begins[:, 0] // key_block
    diag = jnp.maximum(low, query_first // key_block)
    mid = jnp.clip((begins[:, -1] + key_block - 1) // key_block, low, diag)
    end = (query_first + query_block + key_block - 1) // key_block
    spec = pltpu.PrefetchScalarGridSpec(
        num_scalar_prefetch=5,
        grid=(blocks,),
        in_specs=[
            pl.BlockSpec((query_block, width), lambda i, *_: (i, 0)),
            pl.BlockSpec(keys_values.shape, lambda i, *_: (0, 0)),
            pl.BlockSpec((query_block, 1), lambda i, *_: (i, 0)),
        ],
        out_specs=pl.BlockSpec((query_block, width), lambda i, *_: (i, 0)),
        scratch_shapes=[
            pltpu.VMEM((query_block, width), jnp.float32),
            pltpu.VMEM((head_count, query_block, HEAD_WIDTH), jnp.float32),
            pltpu.VMEM((head_count, query_block, HEAD_WIDTH), jnp.float32),
        ],
    )
    pairs = tokens * keys_values.shape[0] * head_count // 2
    return pl.pallas_call(
        functools.partial(attention_kernel, head_count, key_block),
        out_shape=jax.ShapeDtypeStruct((tokens, width), jnp.bfloat16),
        grid_spec=spec,
        compiler_params=pltpu.CompilerParams(vmem_limit_bytes=48 * 1024 * 1024),
        cost_estimate=pl.CostEstimate(
            flops=4 * pairs * HEAD_WIDTH, bytes_accessed=8 << 20, transcendentals=pairs
        ),
    )(low, mid, diag, end, jnp.reshape(first, (1,)), queries, keys_values, starts[:, None])


def plane_local(tokens, norm_gain, wq, wk, wv, wo, doc_ids):
    tok_rows, model_width = tokens.shape
    plane = lax.axis_size("h")
    planes = lax.axis_size("z")
    first_pos = lax.axis_index("z") * (tok_rows * plane)
    source = tokens.astype(jnp.float32)
    mean_sq = jnp.mean(source * source, axis=1, keepdims=True)
    normed = (source * lax.rsqrt(mean_sq + 1e-05) * norm_gain[None, :]).astype(jnp.bfloat16)

    wkv = jnp.concatenate(
        [wk.reshape(-1, plane, HEAD_WIDTH), wv.reshape(-1, plane, HEAD_WIDTH)], axis=2
    ).reshape(wk.shape[0], -1)
    wkv_mine = lax.all_to_all(wkv, "h", 1, 0, tiled=True)
    wq_mine = lax.all_to_all(wq, "h", 1, 0, tiled=True)
    normed_all = lax.all_gather(normed, "h", axis=0, tiled=True)
    wkv_all = lax.all_gather(wkv_mine, "z", axis=0, tiled=True)
    wq_all = lax.all_gather(wq_mine, "z", axis=0, tiled=True)
    doc_plane = lax.all_gather(doc_ids, "h", axis=0, tiled=True)
    doc_all = lax.all_gather(doc_plane, "z", axis=0, tiled=True)

    plane_rows = tok_rows * plane
    positions = first_pos + jnp.arange(plane_rows, dtype=jnp.int32)
    doc_mine = doc_plane
    starts = jnp.sum((doc_all[None, :] < doc_mine[:, None]).astype(jnp.int32), axis=1)

    kv_acc = jnp.dot(normed_all, wkv_all, preferred_element_type=jnp.float32)
    keys = rope(kv_acc[:, None, :HEAD_WIDTH], positions)[:, 0]
    kv_mine = jnp.concatenate([keys, kv_acc[:, HEAD_WIDTH:]], axis=1).astype(jnp.bfloat16)
    kv_all = lax.all_gather(kv_mine, "z", axis=0, tiled=True)

    query_acc = jnp.dot(normed_all, wq_all, preferred_element_type=jnp.float32)
    queries = rope(query_acc.reshape(plane_rows, -1, HEAD_WIDTH), positions)
    queries = queries.astype(jnp.bfloat16).reshape(plane_rows, -1)

    wo_all = lax.all_gather(wo, "z", axis=1, tiled=True)
    attended = attend(queries, kv_all, starts, first_pos, 256, 512)
    attended_all = lax.all_gather(attended, "h", axis=1, tiled=True)
    terms = jnp.dot(attended_all, wo_all, preferred_element_type=jnp.float32).astype(jnp.bfloat16)
    rows_mine = lax.all_to_all(terms, "h", 0, 1, tiled=True)
    summed = rows_mine.reshape(tok_rows, plane, planes, -1).transpose(0, 2, 1, 3)
    summed = summed.reshape(tok_rows, model_width).astype(jnp.float32)
    return (source + summed).astype(jnp.bfloat16)


def plane_solution(mesh, planes):
    folded = jax.sharding.Mesh(mesh.devices.reshape(planes, KV_HEAD_COUNT), ("z", "h"))
    rows = P(("z", "h"))
    return jax.shard_map(
        plane_local,
        mesh=folded,
        in_specs=(rows, P(), rows, rows, rows, P(None, ("z", "h")), rows),
        out_specs=rows,
        check_vma=False,
    )


def solution(mesh):
    if mesh.shape["grp"] == 1 and mesh.shape["head"] == 1 and mesh.size % KV_HEAD_COUNT == 0:
        return plane_solution(mesh, mesh.size // KV_HEAD_COUNT)
    in_specs = (
        P(("grp", "seq", "srv"), "head"),
        P(),
        P(("seq", "srv"), "head"),
        P(("seq", "srv"), "head"),
        P(("seq", "srv"), "head"),
        P("head", ("seq", "srv")),
        P(("grp", "seq", "srv")),
    )
    out_specs = P(("grp", "seq", "srv"), "head")
    return jax.shard_map(local, mesh=mesh, in_specs=in_specs, out_specs=out_specs, check_vma=False)
```

```python
import functools
import math

import jax
import jax.numpy as jnp
from jax import lax
from jax.experimental import pallas as pl
from jax.experimental.pallas import tpu as pltpu
from jax.sharding import PartitionSpec as P

QUERY_HEADS = 32
KV_HEAD_COUNT = 8
HEAD_WIDTH = 128


def rope(field, positions):
    half = field.shape[-1] // 2
    freqs = 500000.0 ** (-(jnp.arange(half, dtype=jnp.float32) * 2.0 / field.shape[-1]))
    angles = positions.astype(jnp.float32)[:, None] * freqs[None, :]
    cosine = jnp.cos(angles)[:, None, :]
    sine = jnp.sin(angles)[:, None, :]
    first = field[..., :half]
    second = field[..., half:]
    return jnp.concatenate(
        [first * cosine - second * sine, second * cosine + first * sine], axis=-1
    )


def local(tokens, norm_gain, wq, wk, wv, wo, doc_ids):
    tok_rows = tokens.shape[0]
    head_size = HEAD_WIDTH
    kv_local = wk.shape[1] // head_size
    query_group = QUERY_HEADS // KV_HEAD_COUNT
    source = tokens.astype(jnp.float32)
    whole = lax.all_gather(tokens, "head", axis=1, tiled=True).astype(jnp.float32)
    mean_sq = jnp.mean(whole * whole, axis=1, keepdims=True)
    normed_input = (whole * lax.rsqrt(mean_sq + 1e-05) * norm_gain[None, :]).astype(jnp.bfloat16)
    query_acc = jnp.dot(
        normed_input,
        lax.all_gather(wq, ("seq", "srv"), axis=0, tiled=True),
        preferred_element_type=jnp.float32,
    )
    key_acc = jnp.dot(
        normed_input,
        lax.all_gather(wk, ("seq", "srv"), axis=0, tiled=True),
        preferred_element_type=jnp.float32,
    )
    value_acc = jnp.dot(
        normed_input,
        lax.all_gather(wv, ("seq", "srv"), axis=0, tiled=True),
        preferred_element_type=jnp.float32,
    )
    first_pos = lax.axis_index(("seq", "srv")) * tok_rows
    positions = first_pos + jnp.arange(tok_rows, dtype=jnp.int32)
    query_matrix = rope(query_acc.reshape(tok_rows, kv_local * query_group, head_size), positions)
    query_matrix = query_matrix.astype(jnp.bfloat16).reshape(
        tok_rows, kv_local, query_group, head_size
    )
    key_matrix = rope(key_acc.reshape(tok_rows, kv_local, head_size), positions).astype(
        jnp.bfloat16
    )
    key_matrix = key_matrix.reshape(tok_rows, kv_local * head_size)
    value_matrix = value_acc.astype(jnp.bfloat16)
    scale = 1.0 / head_size**0.5

    def attend_block(carry, key_rows, value_rows, doc_rows, key_pos):
        run_top, run_total, run_acc = carry
        key_heads = key_rows.reshape(key_rows.shape[0], kv_local, head_size)
        value_heads = value_rows.reshape(value_rows.shape[0], kv_local, head_size)
        scores = (
            jnp.einsum(
                "qcgd,kcd->qcgk", query_matrix, key_heads, preferred_element_type=jnp.float32
            )
            * scale
        )
        allowed = (
            (key_pos[None, :] <= positions[:, None])
            & (key_pos[None, :] >= 0)
            & (doc_rows[None, :] == doc_ids[:, None])
        )
        allowed = allowed[:, None, None, :]
        masked = jnp.where(allowed, scores, -1e30)
        new_top = jnp.maximum(run_top, jnp.max(masked, axis=3))
        expd = jnp.where(allowed, jnp.exp(masked - new_top[..., None]), 0.0)
        factor = jnp.exp(run_top - new_top)
        new_total = run_total * factor + jnp.sum(expd, axis=3)
        weights = expd.astype(jnp.bfloat16)
        update = jnp.einsum(
            "qcgk,kcd->qcgd", weights, value_heads, preferred_element_type=jnp.float32
        )
        return (new_top, new_total, run_acc * factor[..., None] + update)

    start_state = (
        jnp.full((tok_rows, kv_local, query_group), -1e30, jnp.float32),
        jnp.zeros((tok_rows, kv_local, query_group), jnp.float32),
        jnp.zeros((tok_rows, kv_local, query_group, head_size), jnp.float32),
    )
    key_piece = lax.all_gather(key_matrix, ("seq", "srv"), axis=0, tiled=True)
    value_piece = lax.all_gather(value_matrix, ("seq", "srv"), axis=0, tiled=True)
    doc_piece = lax.all_gather(doc_ids, ("seq", "srv"), axis=0, tiled=True)
    count = key_piece.shape[0]
    width = math.gcd(count, 512)

    def step(inner, index):
        offset = index * width
        key_rows = lax.dynamic_slice_in_dim(key_piece, offset, width, 0)
        value_rows = lax.dynamic_slice_in_dim(value_piece, offset, width, 0)
        doc_rows = lax.dynamic_slice_in_dim(doc_piece, offset, width, 0)
        key_pos = offset + jnp.arange(width, dtype=jnp.int32)
        return (attend_block(inner, key_rows, value_rows, doc_rows, key_pos), None)

    def run_all(inner):
        result, unused = lax.scan(step, inner, jnp.arange(count // width, dtype=jnp.int32))
        return result

    beyond = jnp.int32(0) > first_pos + tok_rows - 1
    before = doc_piece[count - 1] < doc_ids[0]
    final_top, final_total, final_acc = lax.cond(
        beyond | before, lambda inner: inner, run_all, start_state
    )
    attended = (final_acc / final_total[..., None]).astype(jnp.bfloat16)
    attended = attended.reshape(tok_rows, kv_local * query_group * head_size)
    terms = jnp.dot(
        attended,
        lax.all_gather(wo, ("seq", "srv"), axis=1, tiled=True),
        preferred_element_type=jnp.float32,
    )
    summed = lax.psum_scatter(
        terms.astype(jnp.bfloat16), "head", scatter_dimension=1, tiled=True
    ).astype(jnp.float32)
    return (source + summed).astype(jnp.bfloat16)


def attention_kernel(head_count, key_block, lo_ref, mid_ref, diag_ref, end_ref, first_ref,
                     q_ref, kv_ref, start_ref, out_ref, acc_ref, top_ref, total_ref):
    block = pl.program_id(0)
    rows = q_ref.shape[0]
    top_ref[...] = jnp.full_like(top_ref, -1e30)
    total_ref[...] = jnp.zeros_like(total_ref)
    acc_ref[...] = jnp.zeros_like(acc_ref)
    factor_log2 = 1.4426950408889634 / HEAD_WIDTH**0.5
    starts = start_ref[...]
    query_pos = (
        first_ref[0] + block * rows + lax.broadcasted_iota(jnp.int32, (rows, key_block), 0)
    )

    def visit(index, masked):
        offset = pl.multiple_of(index * key_block, key_block)
        keys = kv_ref[pl.ds(offset, key_block), :HEAD_WIDTH]
        values = kv_ref[pl.ds(offset, key_block), HEAD_WIDTH:]
        if masked:
            key_pos = offset + lax.broadcasted_iota(jnp.int32, (rows, key_block), 1)
            allowed = (key_pos <= query_pos) & (key_pos >= starts)
        for head in range(head_count):
            columns = slice(head * HEAD_WIDTH, (head + 1) * HEAD_WIDTH)
            scores = lax.dot_general(
                q_ref[:, columns], keys, (((1,), (1,)), ((), ())),
                preferred_element_type=jnp.float32,
            )
            if masked:
                scores = jnp.where(allowed, scores, -1e30)
            old_top = top_ref[head]
            new_top = jnp.maximum(old_top, jnp.max(scores, axis=1, keepdims=True))
            expd = jnp.exp2((scores - new_top[:, :1]) * factor_log2)
            factor = jnp.exp2((old_top - new_top) * factor_log2)
            top_ref[head] = new_top
            total_ref[head] = total_ref[head] * factor + jnp.sum(expd, axis=1, keepdims=True)
            acc_ref[:, columns] = acc_ref[:, columns] * factor + jnp.dot(
                expd.astype(jnp.bfloat16), values, preferred_element_type=jnp.float32
            )

    low, mid, diag, end = lo_ref[block], mid_ref[block], diag_ref[block], end_ref[block]

    @pl.loop(low, mid)
    def _(index):
        visit(index, True)

    @pl.loop(mid, diag)
    def _(index):
        visit(index, False)

    @pl.loop(diag, end)
    def _(index):
        visit(index, True)

    for head in range(head_count):
        columns = slice(head * HEAD_WIDTH, (head + 1) * HEAD_WIDTH)
        out_ref[:, columns] = (acc_ref[:, columns] / total_ref[head]).astype(jnp.bfloat16)


def attend(queries, keys_values, starts, first, query_block, key_block):
    tokens, width = queries.shape
    blocks = tokens // query_block
    head_count = width // HEAD_WIDTH
    begins = starts.reshape(blocks, query_block)
    query_first = first + jnp.arange(blocks, dtype=jnp.int32) * query_block
    low = begins[:, 0] // key_block
    diag = jnp.maximum(low, query_first // key_block)
    mid = jnp.clip((begins[:, -1] + key_block - 1) // key_block, low, diag)
    end = (query_first + query_block + key_block - 1) // key_block
    spec = pltpu.PrefetchScalarGridSpec(
        num_scalar_prefetch=5,
        grid=(blocks,),
        in_specs=[
            pl.BlockSpec((query_block, width), lambda i, *_: (i, 0)),
            pl.BlockSpec(keys_values.shape, lambda i, *_: (0, 0)),
            pl.BlockSpec((query_block, 1), lambda i, *_: (i, 0)),
        ],
        out_specs=pl.BlockSpec((query_block, width), lambda i, *_: (i, 0)),
        scratch_shapes=[
            pltpu.VMEM((query_block, width), jnp.float32),
            pltpu.VMEM((head_count, query_block, HEAD_WIDTH), jnp.float32),
            pltpu.VMEM((head_count, query_block, HEAD_WIDTH), jnp.float32),
        ],
    )
    pairs = tokens * keys_values.shape[0] * head_count // 2
    return pl.pallas_call(
        functools.partial(attention_kernel, head_count, key_block),
        out_shape=jax.ShapeDtypeStruct((tokens, width), jnp.bfloat16),
        grid_spec=spec,
        compiler_params=pltpu.CompilerParams(vmem_limit_bytes=48 * 1024 * 1024),
        cost_estimate=pl.CostEstimate(
            flops=32 * pairs * HEAD_WIDTH, bytes_accessed=128 << 20, transcendentals=pairs
        ),
    )(low, mid, diag, end, jnp.reshape(first, (1,)), queries, keys_values, starts[:, None])


def plane_local(tokens, norm_gain, wq, wk, wv, wo, doc_ids):
    tok_rows, model_width = tokens.shape
    plane = lax.axis_size("h")
    planes = lax.axis_size("z")
    first_pos = lax.axis_index("z") * (tok_rows * plane)
    source = tokens.astype(jnp.float32)
    mean_sq = jnp.mean(source * source, axis=1, keepdims=True)
    normed = (source * lax.rsqrt(mean_sq + 1e-05) * norm_gain[None, :]).astype(jnp.bfloat16)

    width = wq.shape[1] // plane
    pack = 16
    pieces = [weight.reshape(tok_rows, plane, -1) for weight in (wq, wk, wv)]
    weights = jnp.concatenate(pieces, axis=2)
    doc_rows = jnp.zeros((pack, plane, weights.shape[2]), jnp.bfloat16)
    doc_rows = doc_rows.at[0, :, :tok_rows].set(doc_ids.astype(jnp.bfloat16))
    sent = jnp.concatenate([weights, doc_rows], axis=0)
    sent, normed = lax.optimization_barrier((sent, normed))
    normed_all = lax.all_gather(normed, "h", axis=0, tiled=True)
    landed = lax.all_to_all(sent.reshape(tok_rows + pack, -1), "h", 1, 0, tiled=True)
    landed = landed.reshape(plane, tok_rows + pack, -1)
    doc_plane = landed[:, tok_rows, :tok_rows].reshape(-1)
    w_mine = landed[:, :tok_rows].reshape(plane * tok_rows, -1)
    w_mine, normed_all = lax.optimization_barrier((w_mine, normed_all))
    w_all = lax.all_gather(w_mine, "z", axis=0, tiled=True)

    plane_rows = tok_rows * plane
    positions = first_pos + jnp.arange(plane_rows, dtype=jnp.int32)

    kv_acc = jnp.dot(normed_all, w_all[:, width:], preferred_element_type=jnp.float32)
    keys = rope(kv_acc[:, None, :HEAD_WIDTH], positions)[:, 0]
    kv_mine = jnp.concatenate([keys, kv_acc[:, HEAD_WIDTH:]], axis=1).astype(jnp.bfloat16)
    doc_fold = doc_plane.reshape(-1, 2 * HEAD_WIDTH)
    doc_fold = jnp.pad(doc_fold, ((0, -doc_fold.shape[0] % pack), (0, 0)))
    kv_docs = lax.all_gather(jnp.concatenate([kv_mine, doc_fold], axis=0), "z", axis=0)
    kv_all = kv_docs[:, :plane_rows].reshape(planes * plane_rows, -1)
    doc_all = kv_docs[:, plane_rows:].reshape(planes, -1)[:, :plane_rows].reshape(-1)
    doc_mine = doc_plane
    starts = jnp.sum((doc_all[None, :] < doc_mine[:, None]).astype(jnp.int32), axis=1)

    query_acc = jnp.dot(normed_all, w_all[:, :width], preferred_element_type=jnp.float32)
    queries = rope(query_acc.reshape(plane_rows, -1, HEAD_WIDTH), positions)
    queries = queries.astype(jnp.bfloat16).reshape(plane_rows, -1)

    wo, kv_all = lax.optimization_barrier((wo, kv_all))
    wo_all = lax.all_gather(wo, "z", axis=1, tiled=True)
    attended = attend(queries, kv_all, starts, first_pos, 256, 512)
    attended, wo_all = lax.optimization_barrier((attended, wo_all))
    attended_all = lax.all_gather(attended, "h", axis=1, tiled=True)
    terms = jnp.dot(attended_all, wo_all, preferred_element_type=jnp.float32).astype(jnp.bfloat16)
    rows_mine = lax.all_to_all(terms, "h", 0, 1, tiled=True)
    summed = rows_mine.reshape(tok_rows, plane, planes, -1).transpose(0, 2, 1, 3)
    summed = summed.reshape(tok_rows, model_width).astype(jnp.float32)
    return (source + summed).astype(jnp.bfloat16)


def plane_solution(mesh, planes):
    folded = jax.sharding.Mesh(mesh.devices.reshape(planes, KV_HEAD_COUNT), ("z", "h"))
    rows = P(("z", "h"))
    return jax.shard_map(
        plane_local,
        mesh=folded,
        in_specs=(rows, P(), rows, rows, rows, P(None, ("z", "h")), rows),
        out_specs=rows,
        check_vma=False,
    )


def solution(mesh):
    if mesh.shape["grp"] == 1 and mesh.shape["head"] == 1 and mesh.size % KV_HEAD_COUNT == 0:
        return plane_solution(mesh, mesh.size // KV_HEAD_COUNT)
    in_specs = (
        P(("grp", "seq", "srv"), "head"),
        P(),
        P(("seq", "srv"), "head"),
        P(("seq", "srv"), "head"),
        P(("seq", "srv"), "head"),
        P("head", ("seq", "srv")),
        P(("grp", "seq", "srv")),
    )
    out_specs = P(("grp", "seq", "srv"), "head")
    return jax.shard_map(local, mesh=mesh, in_specs=in_specs, out_specs=out_specs, check_vma=False)
```

```python
import functools
import math

import jax
import jax.numpy as jnp
from jax import lax
from jax.experimental import pallas as pl
from jax.experimental.pallas import tpu as pltpu
from jax.sharding import PartitionSpec as P

QUERY_HEADS = 32
KV_HEAD_COUNT = 8
HEAD_WIDTH = 128


def rope(field, positions):
    half = field.shape[-1] // 2
    freqs = 500000.0 ** (-(jnp.arange(half, dtype=jnp.float32) * 2.0 / field.shape[-1]))
    angles = positions.astype(jnp.float32)[:, None] * freqs[None, :]
    cosine = jnp.cos(angles)[:, None, :]
    sine = jnp.sin(angles)[:, None, :]
    first = field[..., :half]
    second = field[..., half:]
    return jnp.concatenate(
        [first * cosine - second * sine, second * cosine + first * sine], axis=-1
    )


def local(tokens, norm_gain, wq, wk, wv, wo, doc_ids):
    tok_rows = tokens.shape[0]
    head_size = HEAD_WIDTH
    kv_local = wk.shape[1] // head_size
    query_group = QUERY_HEADS // KV_HEAD_COUNT
    source = tokens.astype(jnp.float32)
    whole = lax.all_gather(tokens, "head", axis=1, tiled=True).astype(jnp.float32)
    mean_sq = jnp.mean(whole * whole, axis=1, keepdims=True)
    normed_input = (whole * lax.rsqrt(mean_sq + 1e-05) * norm_gain[None, :]).astype(jnp.bfloat16)
    query_acc = jnp.dot(
        normed_input,
        lax.all_gather(wq, ("seq", "srv"), axis=0, tiled=True),
        preferred_element_type=jnp.float32,
    )
    key_acc = jnp.dot(
        normed_input,
        lax.all_gather(wk, ("seq", "srv"), axis=0, tiled=True),
        preferred_element_type=jnp.float32,
    )
    value_acc = jnp.dot(
        normed_input,
        lax.all_gather(wv, ("seq", "srv"), axis=0, tiled=True),
        preferred_element_type=jnp.float32,
    )
    first_pos = lax.axis_index(("seq", "srv")) * tok_rows
    positions = first_pos + jnp.arange(tok_rows, dtype=jnp.int32)
    query_matrix = rope(query_acc.reshape(tok_rows, kv_local * query_group, head_size), positions)
    query_matrix = query_matrix.astype(jnp.bfloat16).reshape(
        tok_rows, kv_local, query_group, head_size
    )
    key_matrix = rope(key_acc.reshape(tok_rows, kv_local, head_size), positions).astype(
        jnp.bfloat16
    )
    key_matrix = key_matrix.reshape(tok_rows, kv_local * head_size)
    value_matrix = value_acc.astype(jnp.bfloat16)
    scale = 1.0 / head_size**0.5

    def attend_block(carry, key_rows, value_rows, doc_rows, key_pos):
        run_top, run_total, run_acc = carry
        key_heads = key_rows.reshape(key_rows.shape[0], kv_local, head_size)
        value_heads = value_rows.reshape(value_rows.shape[0], kv_local, head_size)
        scores = (
            jnp.einsum(
                "qcgd,kcd->qcgk", query_matrix, key_heads, preferred_element_type=jnp.float32
            )
            * scale
        )
        allowed = (
            (key_pos[None, :] <= positions[:, None])
            & (key_pos[None, :] >= 0)
            & (doc_rows[None, :] == doc_ids[:, None])
        )
        allowed = allowed[:, None, None, :]
        masked = jnp.where(allowed, scores, -1e30)
        new_top = jnp.maximum(run_top, jnp.max(masked, axis=3))
        expd = jnp.where(allowed, jnp.exp(masked - new_top[..., None]), 0.0)
        factor = jnp.exp(run_top - new_top)
        new_total = run_total * factor + jnp.sum(expd, axis=3)
        weights = expd.astype(jnp.bfloat16)
        update = jnp.einsum(
            "qcgk,kcd->qcgd", weights, value_heads, preferred_element_type=jnp.float32
        )
        return (new_top, new_total, run_acc * factor[..., None] + update)

    start_state = (
        jnp.full((tok_rows, kv_local, query_group), -1e30, jnp.float32),
        jnp.zeros((tok_rows, kv_local, query_group), jnp.float32),
        jnp.zeros((tok_rows, kv_local, query_group, head_size), jnp.float32),
    )
    key_piece = lax.all_gather(key_matrix, ("seq", "srv"), axis=0, tiled=True)
    value_piece = lax.all_gather(value_matrix, ("seq", "srv"), axis=0, tiled=True)
    doc_piece = lax.all_gather(doc_ids, ("seq", "srv"), axis=0, tiled=True)
    count = key_piece.shape[0]
    width = math.gcd(count, 512)

    def step(inner, index):
        offset = index * width
        key_rows = lax.dynamic_slice_in_dim(key_piece, offset, width, 0)
        value_rows = lax.dynamic_slice_in_dim(value_piece, offset, width, 0)
        doc_rows = lax.dynamic_slice_in_dim(doc_piece, offset, width, 0)
        key_pos = offset + jnp.arange(width, dtype=jnp.int32)
        return (attend_block(inner, key_rows, value_rows, doc_rows, key_pos), None)

    def run_all(inner):
        result, unused = lax.scan(step, inner, jnp.arange(count // width, dtype=jnp.int32))
        return result

    beyond = jnp.int32(0) > first_pos + tok_rows - 1
    before = doc_piece[count - 1] < doc_ids[0]
    final_top, final_total, final_acc = lax.cond(
        beyond | before, lambda inner: inner, run_all, start_state
    )
    attended = (final_acc / final_total[..., None]).astype(jnp.bfloat16)
    attended = attended.reshape(tok_rows, kv_local * query_group * head_size)
    terms = jnp.dot(
        attended,
        lax.all_gather(wo, ("seq", "srv"), axis=1, tiled=True),
        preferred_element_type=jnp.float32,
    )
    summed = lax.psum_scatter(
        terms.astype(jnp.bfloat16), "head", scatter_dimension=1, tiled=True
    ).astype(jnp.float32)
    return (source + summed).astype(jnp.bfloat16)


def attention_kernel(head_count, key_block, lo_ref, mid_ref, diag_ref, end_ref, first_ref,
                     q_ref, kv_ref, start_ref, out_ref, acc_ref, top_ref, total_ref):
    block = pl.program_id(0)
    rows = q_ref.shape[0]
    top_ref[...] = jnp.full_like(top_ref, -1e30)
    total_ref[...] = jnp.zeros_like(total_ref)
    acc_ref[...] = jnp.zeros_like(acc_ref)
    factor_log2 = 1.4426950408889634 / HEAD_WIDTH**0.5
    starts = start_ref[...]
    query_pos = (
        first_ref[0] + block * rows + lax.broadcasted_iota(jnp.int32, (rows, key_block), 0)
    )

    def visit(index, masked):
        offset = pl.multiple_of(index * key_block, key_block)
        keys = kv_ref[pl.ds(offset, key_block), :HEAD_WIDTH]
        values = kv_ref[pl.ds(offset, key_block), HEAD_WIDTH:]
        if masked:
            key_pos = offset + lax.broadcasted_iota(jnp.int32, (rows, key_block), 1)
            allowed = (key_pos <= query_pos) & (key_pos >= starts)
        for head in range(head_count):
            columns = slice(head * HEAD_WIDTH, (head + 1) * HEAD_WIDTH)
            scores = lax.dot_general(
                q_ref[:, columns], keys, (((1,), (1,)), ((), ())),
                preferred_element_type=jnp.float32,
            )
            if masked:
                scores = jnp.where(allowed, scores, -1e30)
            old_top = top_ref[head]
            new_top = jnp.maximum(old_top, jnp.max(scores, axis=1, keepdims=True))
            expd = jnp.exp2((scores - new_top[:, :1]) * factor_log2)
            factor = jnp.exp2((old_top - new_top) * factor_log2)
            top_ref[head] = new_top
            total_ref[head] = total_ref[head] * factor + jnp.sum(expd, axis=1, keepdims=True)
            acc_ref[:, columns] = acc_ref[:, columns] * factor + jnp.dot(
                expd.astype(jnp.bfloat16), values, preferred_element_type=jnp.float32
            )

    low, mid, diag, end = lo_ref[block], mid_ref[block], diag_ref[block], end_ref[block]

    @pl.loop(low, mid)
    def _(index):
        visit(index, True)

    @pl.loop(mid, diag)
    def _(index):
        visit(index, False)

    @pl.loop(diag, end)
    def _(index):
        visit(index, True)

    for head in range(head_count):
        columns = slice(head * HEAD_WIDTH, (head + 1) * HEAD_WIDTH)
        out_ref[:, columns] = (acc_ref[:, columns] / total_ref[head]).astype(jnp.bfloat16)


def attend(queries, keys_values, starts, first, query_block, key_block):
    tokens, width = queries.shape
    blocks = tokens // query_block
    head_count = width // HEAD_WIDTH
    begins = starts.reshape(blocks, query_block)
    query_first = first + jnp.arange(blocks, dtype=jnp.int32) * query_block
    low = begins[:, 0] // key_block
    diag = jnp.maximum(low, query_first // key_block)
    mid = jnp.clip((begins[:, -1] + key_block - 1) // key_block, low, diag)
    end = (query_first + query_block + key_block - 1) // key_block
    spec = pltpu.PrefetchScalarGridSpec(
        num_scalar_prefetch=5,
        grid=(blocks,),
        in_specs=[
            pl.BlockSpec((query_block, width), lambda i, *_: (i, 0)),
            pl.BlockSpec(keys_values.shape, lambda i, *_: (0, 0)),
            pl.BlockSpec((query_block, 1), lambda i, *_: (i, 0)),
        ],
        out_specs=pl.BlockSpec((query_block, width), lambda i, *_: (i, 0)),
        scratch_shapes=[
            pltpu.VMEM((query_block, width), jnp.float32),
            pltpu.VMEM((head_count, query_block, HEAD_WIDTH), jnp.float32),
            pltpu.VMEM((head_count, query_block, HEAD_WIDTH), jnp.float32),
        ],
    )
    pairs = tokens * keys_values.shape[0] * head_count // 2
    return pl.pallas_call(
        functools.partial(attention_kernel, head_count, key_block),
        out_shape=jax.ShapeDtypeStruct((tokens, width), jnp.bfloat16),
        grid_spec=spec,
        compiler_params=pltpu.CompilerParams(vmem_limit_bytes=48 * 1024 * 1024),
        cost_estimate=pl.CostEstimate(
            flops=32 * pairs * HEAD_WIDTH, bytes_accessed=128 << 20, transcendentals=pairs
        ),
    )(low, mid, diag, end, jnp.reshape(first, (1,)), queries, keys_values, starts[:, None])


def permuted(block, axis, partner):
    count = lax.axis_size(axis)
    return [
        lax.ppermute(block, axis, [(i, partner(i, k)) for i in range(count)])
        for k in range(1, count)
    ]


def laid(blocks, origins, dim):
    size = blocks[0].shape[dim]
    shape = list(blocks[0].shape)
    shape[dim] = size * len(blocks)
    whole = jnp.zeros(shape, blocks[0].dtype)
    for block, origin in zip(blocks, origins):
        whole = lax.dynamic_update_slice_in_dim(whole, block, origin * size, dim)
    return whole


def plane_local(tokens, norm_gain, wq, wk, wv, wo, doc_ids):
    tok_rows, model_width = tokens.shape
    plane = lax.axis_size("h")
    planes = lax.axis_size("z")
    first_pos = lax.axis_index("z") * (tok_rows * plane)
    source = tokens.astype(jnp.float32)
    mean_sq = jnp.mean(source * source, axis=1, keepdims=True)
    normed = (source * lax.rsqrt(mean_sq + 1e-05) * norm_gain[None, :]).astype(jnp.bfloat16)

    width = wq.shape[1] // plane
    pack = 16
    pieces = [weight.reshape(tok_rows, plane, -1) for weight in (wq, wk, wv)]
    weights = jnp.concatenate(pieces, axis=2)
    doc_rows = jnp.zeros((pack, plane, weights.shape[2]), jnp.bfloat16)
    doc_rows = doc_rows.at[0, :, :tok_rows].set(doc_ids.astype(jnp.bfloat16))
    sent = jnp.concatenate([weights, doc_rows], axis=0)
    sent, normed = lax.optimization_barrier((sent, normed))
    me = lax.axis_index("h")
    normed_blocks = [normed] + permuted(normed, "h", lambda i, k: i ^ k)
    normed_all = laid(normed_blocks, [me ^ k for k in range(plane)], 0)
    landed = lax.all_to_all(sent.reshape(tok_rows + pack, -1), "h", 1, 0, tiled=True)
    landed = landed.reshape(plane, tok_rows + pack, -1)
    doc_plane = landed[:, tok_rows, :tok_rows].reshape(-1)
    w_mine = landed[:, :tok_rows].reshape(plane * tok_rows, -1)
    w_all = lax.all_gather(w_mine, "z", axis=0, tiled=True)

    plane_rows = tok_rows * plane
    positions = first_pos + jnp.arange(plane_rows, dtype=jnp.int32)

    kv_acc = jnp.dot(normed_all, w_all[:, width:], preferred_element_type=jnp.float32)
    keys = rope(kv_acc[:, None, :HEAD_WIDTH], positions)[:, 0]
    kv_mine = jnp.concatenate([keys, kv_acc[:, HEAD_WIDTH:]], axis=1).astype(jnp.bfloat16)
    doc_fold = doc_plane.reshape(-1, 2 * HEAD_WIDTH)
    doc_fold = jnp.pad(doc_fold, ((0, -doc_fold.shape[0] % pack), (0, 0)))
    kv_docs = lax.all_gather(jnp.concatenate([kv_mine, doc_fold], axis=0), "z", axis=0)
    kv_all = kv_docs[:, :plane_rows].reshape(planes * plane_rows, -1)
    doc_all = kv_docs[:, plane_rows:].reshape(planes, -1)[:, :plane_rows].reshape(-1)
    doc_mine = doc_plane
    starts = jnp.sum((doc_all[None, :] < doc_mine[:, None]).astype(jnp.int32), axis=1)

    query_acc = jnp.dot(normed_all, w_all[:, :width], preferred_element_type=jnp.float32)
    queries = rope(query_acc.reshape(plane_rows, -1, HEAD_WIDTH), positions)
    queries = queries.astype(jnp.bfloat16).reshape(plane_rows, -1)

    wo, kv_all, starts, queries = lax.optimization_barrier((wo, kv_all, starts, queries))
    moved = permuted(wo, "z", lambda i, k: (i + k) % planes)
    attended = attend(queries, kv_all, starts, first_pos, 256, 512)
    attended, moved[0], moved[-1] = lax.optimization_barrier((attended, moved[0], moved[-1]))
    level = lax.axis_index("z")
    wo_all = laid([wo] + moved, [(level - k) % planes for k in range(planes)], 1)
    attended_all = lax.all_gather(attended, "h", axis=1, tiled=True)
    terms = jnp.dot(attended_all, wo_all, preferred_element_type=jnp.float32).astype(jnp.bfloat16)
    rows_mine = lax.all_to_all(terms, "h", 0, 1, tiled=True)
    summed = rows_mine.reshape(tok_rows, plane, planes, -1).transpose(0, 2, 1, 3)
    summed = summed.reshape(tok_rows, model_width).astype(jnp.float32)
    return (source + summed).astype(jnp.bfloat16)


def plane_solution(mesh, planes):
    folded = jax.sharding.Mesh(mesh.devices.reshape(planes, KV_HEAD_COUNT), ("z", "h"))
    rows = P(("z", "h"))
    return jax.shard_map(
        plane_local,
        mesh=folded,
        in_specs=(rows, P(), rows, rows, rows, P(None, ("z", "h")), rows),
        out_specs=rows,
        check_vma=False,
    )


def solution(mesh):
    if mesh.shape["grp"] == 1 and mesh.shape["head"] == 1 and mesh.size % KV_HEAD_COUNT == 0:
        return plane_solution(mesh, mesh.size // KV_HEAD_COUNT)
    in_specs = (
        P(("grp", "seq", "srv"), "head"),
        P(),
        P(("seq", "srv"), "head"),
        P(("seq", "srv"), "head"),
        P(("seq", "srv"), "head"),
        P("head", ("seq", "srv")),
        P(("grp", "seq", "srv")),
    )
    out_specs = P(("grp", "seq", "srv"), "head")
    return jax.shard_map(local, mesh=mesh, in_specs=in_specs, out_specs=out_specs, check_vma=False)
```

```python
import functools
import math

import jax
import jax.numpy as jnp
from jax import lax
from jax.experimental import pallas as pl
from jax.experimental.pallas import tpu as pltpu
from jax.sharding import PartitionSpec as P

QUERY_HEADS = 32
KV_HEAD_COUNT = 8
HEAD_WIDTH = 128


def rope(field, positions):
    half = field.shape[-1] // 2
    freqs = 500000.0 ** (-(jnp.arange(half, dtype=jnp.float32) * 2.0 / field.shape[-1]))
    angles = positions.astype(jnp.float32)[:, None] * freqs[None, :]
    cosine = jnp.cos(angles)[:, None, :]
    sine = jnp.sin(angles)[:, None, :]
    first = field[..., :half]
    second = field[..., half:]
    return jnp.concatenate(
        [first * cosine - second * sine, second * cosine + first * sine], axis=-1
    )


def local(tokens, norm_gain, wq, wk, wv, wo, doc_ids):
    tok_rows = tokens.shape[0]
    head_size = HEAD_WIDTH
    kv_local = wk.shape[1] // head_size
    query_group = QUERY_HEADS // KV_HEAD_COUNT
    source = tokens.astype(jnp.float32)
    whole = lax.all_gather(tokens, "head", axis=1, tiled=True).astype(jnp.float32)
    mean_sq = jnp.mean(whole * whole, axis=1, keepdims=True)
    normed_input = (whole * lax.rsqrt(mean_sq + 1e-05) * norm_gain[None, :]).astype(jnp.bfloat16)
    query_acc = jnp.dot(
        normed_input,
        lax.all_gather(wq, ("seq", "srv"), axis=0, tiled=True),
        preferred_element_type=jnp.float32,
    )
    key_acc = jnp.dot(
        normed_input,
        lax.all_gather(wk, ("seq", "srv"), axis=0, tiled=True),
        preferred_element_type=jnp.float32,
    )
    value_acc = jnp.dot(
        normed_input,
        lax.all_gather(wv, ("seq", "srv"), axis=0, tiled=True),
        preferred_element_type=jnp.float32,
    )
    first_pos = lax.axis_index(("seq", "srv")) * tok_rows
    positions = first_pos + jnp.arange(tok_rows, dtype=jnp.int32)
    query_matrix = rope(query_acc.reshape(tok_rows, kv_local * query_group, head_size), positions)
    query_matrix = query_matrix.astype(jnp.bfloat16).reshape(
        tok_rows, kv_local, query_group, head_size
    )
    key_matrix = rope(key_acc.reshape(tok_rows, kv_local, head_size), positions).astype(
        jnp.bfloat16
    )
    key_matrix = key_matrix.reshape(tok_rows, kv_local * head_size)
    value_matrix = value_acc.astype(jnp.bfloat16)
    scale = 1.0 / head_size**0.5

    def attend_block(carry, key_rows, value_rows, doc_rows, key_pos):
        run_top, run_total, run_acc = carry
        key_heads = key_rows.reshape(key_rows.shape[0], kv_local, head_size)
        value_heads = value_rows.reshape(value_rows.shape[0], kv_local, head_size)
        scores = (
            jnp.einsum(
                "qcgd,kcd->qcgk", query_matrix, key_heads, preferred_element_type=jnp.float32
            )
            * scale
        )
        allowed = (
            (key_pos[None, :] <= positions[:, None])
            & (key_pos[None, :] >= 0)
            & (doc_rows[None, :] == doc_ids[:, None])
        )
        allowed = allowed[:, None, None, :]
        masked = jnp.where(allowed, scores, -1e30)
        new_top = jnp.maximum(run_top, jnp.max(masked, axis=3))
        expd = jnp.where(allowed, jnp.exp(masked - new_top[..., None]), 0.0)
        factor = jnp.exp(run_top - new_top)
        new_total = run_total * factor + jnp.sum(expd, axis=3)
        weights = expd.astype(jnp.bfloat16)
        update = jnp.einsum(
            "qcgk,kcd->qcgd", weights, value_heads, preferred_element_type=jnp.float32
        )
        return (new_top, new_total, run_acc * factor[..., None] + update)

    start_state = (
        jnp.full((tok_rows, kv_local, query_group), -1e30, jnp.float32),
        jnp.zeros((tok_rows, kv_local, query_group), jnp.float32),
        jnp.zeros((tok_rows, kv_local, query_group, head_size), jnp.float32),
    )
    key_piece = lax.all_gather(key_matrix, ("seq", "srv"), axis=0, tiled=True)
    value_piece = lax.all_gather(value_matrix, ("seq", "srv"), axis=0, tiled=True)
    doc_piece = lax.all_gather(doc_ids, ("seq", "srv"), axis=0, tiled=True)
    count = key_piece.shape[0]
    width = math.gcd(count, 512)

    def step(inner, index):
        offset = index * width
        key_rows = lax.dynamic_slice_in_dim(key_piece, offset, width, 0)
        value_rows = lax.dynamic_slice_in_dim(value_piece, offset, width, 0)
        doc_rows = lax.dynamic_slice_in_dim(doc_piece, offset, width, 0)
        key_pos = offset + jnp.arange(width, dtype=jnp.int32)
        return (attend_block(inner, key_rows, value_rows, doc_rows, key_pos), None)

    def run_all(inner):
        result, unused = lax.scan(step, inner, jnp.arange(count // width, dtype=jnp.int32))
        return result

    beyond = jnp.int32(0) > first_pos + tok_rows - 1
    before = doc_piece[count - 1] < doc_ids[0]
    final_top, final_total, final_acc = lax.cond(
        beyond | before, lambda inner: inner, run_all, start_state
    )
    attended = (final_acc / final_total[..., None]).astype(jnp.bfloat16)
    attended = attended.reshape(tok_rows, kv_local * query_group * head_size)
    terms = jnp.dot(
        attended,
        lax.all_gather(wo, ("seq", "srv"), axis=1, tiled=True),
        preferred_element_type=jnp.float32,
    )
    summed = lax.psum_scatter(
        terms.astype(jnp.bfloat16), "head", scatter_dimension=1, tiled=True
    ).astype(jnp.float32)
    return (source + summed).astype(jnp.bfloat16)


def attention_kernel(head_count, key_block, lo_ref, mid_ref, diag_ref, end_ref, first_ref,
                     q_ref, kv_ref, start_ref, out_ref, acc_ref, top_ref, total_ref):
    block = pl.program_id(0)
    rows = q_ref.shape[0]
    top_ref[...] = jnp.full_like(top_ref, -1e30)
    total_ref[...] = jnp.zeros_like(total_ref)
    acc_ref[...] = jnp.zeros_like(acc_ref)
    factor_log2 = 1.4426950408889634 / HEAD_WIDTH**0.5
    starts = start_ref[...]
    query_pos = (
        first_ref[0] + block * rows + lax.broadcasted_iota(jnp.int32, (rows, key_block), 0)
    )

    def visit(index, masked):
        offset = pl.multiple_of(index * key_block, key_block)
        keys = kv_ref[pl.ds(offset, key_block), :HEAD_WIDTH]
        values = kv_ref[pl.ds(offset, key_block), HEAD_WIDTH:]
        if masked:
            key_pos = offset + lax.broadcasted_iota(jnp.int32, (rows, key_block), 1)
            allowed = (key_pos <= query_pos) & (key_pos >= starts)
        for head in range(head_count):
            columns = slice(head * HEAD_WIDTH, (head + 1) * HEAD_WIDTH)
            scores = lax.dot_general(
                q_ref[:, columns], keys, (((1,), (1,)), ((), ())),
                preferred_element_type=jnp.float32,
            )
            if masked:
                scores = jnp.where(allowed, scores, -1e30)
            old_top = top_ref[head]
            new_top = jnp.maximum(old_top, jnp.max(scores, axis=1, keepdims=True))
            expd = jnp.exp2((scores - new_top[:, :1]) * factor_log2)
            factor = jnp.exp2((old_top - new_top) * factor_log2)
            top_ref[head] = new_top
            total_ref[head] = total_ref[head] * factor + jnp.sum(expd, axis=1, keepdims=True)
            acc_ref[:, columns] = acc_ref[:, columns] * factor + jnp.dot(
                expd.astype(jnp.bfloat16), values, preferred_element_type=jnp.float32
            )

    low, mid, diag, end = lo_ref[block], mid_ref[block], diag_ref[block], end_ref[block]

    @pl.loop(low, mid)
    def _(index):
        visit(index, True)

    @pl.loop(mid, diag)
    def _(index):
        visit(index, False)

    @pl.loop(diag, end)
    def _(index):
        visit(index, True)

    for head in range(head_count):
        columns = slice(head * HEAD_WIDTH, (head + 1) * HEAD_WIDTH)
        out_ref[:, columns] = (acc_ref[:, columns] / total_ref[head]).astype(jnp.bfloat16)


def attend(queries, keys_values, starts, first, query_block, key_block):
    tokens, width = queries.shape
    blocks = tokens // query_block
    head_count = width // HEAD_WIDTH
    begins = starts.reshape(blocks, query_block)
    query_first = first + jnp.arange(blocks, dtype=jnp.int32) * query_block
    low = begins[:, 0] // key_block
    diag = jnp.maximum(low, query_first // key_block)
    mid = jnp.clip((begins[:, -1] + key_block - 1) // key_block, low, diag)
    end = (query_first + query_block + key_block - 1) // key_block
    spec = pltpu.PrefetchScalarGridSpec(
        num_scalar_prefetch=5,
        grid=(blocks,),
        in_specs=[
            pl.BlockSpec((query_block, width), lambda i, *_: (i, 0)),
            pl.BlockSpec(keys_values.shape, lambda i, *_: (0, 0)),
            pl.BlockSpec((query_block, 1), lambda i, *_: (i, 0)),
        ],
        out_specs=pl.BlockSpec((query_block, width), lambda i, *_: (i, 0)),
        scratch_shapes=[
            pltpu.VMEM((query_block, width), jnp.float32),
            pltpu.VMEM((head_count, query_block, HEAD_WIDTH), jnp.float32),
            pltpu.VMEM((head_count, query_block, HEAD_WIDTH), jnp.float32),
        ],
    )
    pairs = tokens * keys_values.shape[0] * head_count // 2
    return pl.pallas_call(
        functools.partial(attention_kernel, head_count, key_block),
        out_shape=jax.ShapeDtypeStruct((tokens, width), jnp.bfloat16),
        grid_spec=spec,
        compiler_params=pltpu.CompilerParams(vmem_limit_bytes=48 * 1024 * 1024),
        cost_estimate=pl.CostEstimate(
            flops=32 * pairs * HEAD_WIDTH, bytes_accessed=64 << 20, transcendentals=pairs
        ),
    )(low, mid, diag, end, jnp.reshape(first, (1,)), queries, keys_values, starts[:, None])


def permuted(block, axis, partner, steps):
    count = lax.axis_size(axis)
    return [
        lax.ppermute(block, axis, [(i, partner(i, k)) for i in range(count)])
        for k in steps
    ]


def laid(blocks, origins, dim):
    size = blocks[0].shape[dim]
    shape = list(blocks[0].shape)
    shape[dim] = size * len(blocks)
    whole = jnp.zeros(shape, blocks[0].dtype)
    for block, origin in zip(blocks, origins):
        whole = lax.dynamic_update_slice_in_dim(whole, block, origin * size, dim)
    return whole


def plane_local(tokens, norm_gain, wq, wk, wv, wo, doc_ids):
    tok_rows, model_width = tokens.shape
    plane = lax.axis_size("h")
    planes = lax.axis_size("z")
    first_pos = lax.axis_index("z") * (tok_rows * plane)
    source = tokens.astype(jnp.float32)
    mean_sq = jnp.mean(source * source, axis=1, keepdims=True)
    normed = (source * lax.rsqrt(mean_sq + 1e-05) * norm_gain[None, :]).astype(jnp.bfloat16)

    width = wq.shape[1] // plane
    pack = 16
    pieces = [weight.reshape(tok_rows, plane, -1) for weight in (wq, wk, wv)]
    weights = jnp.concatenate(pieces, axis=2)
    doc_rows = jnp.zeros((pack, plane, weights.shape[2]), jnp.bfloat16)
    doc_rows = doc_rows.at[0, :, :tok_rows].set(doc_ids.astype(jnp.bfloat16))
    sent = jnp.concatenate([weights, doc_rows], axis=0)
    sent, normed = lax.optimization_barrier((sent, normed))
    me = lax.axis_index("h")
    normed_blocks = [normed] + permuted(normed, "h", lambda i, k: i ^ k, range(1, plane))
    normed_all = laid(normed_blocks, [me ^ k for k in range(plane)], 0)
    landed = lax.all_to_all(sent.reshape(tok_rows + pack, -1), "h", 1, 0, tiled=True)
    ahead = lambda i, k: (i + k) % planes
    outer = permuted(wo, "z", ahead, (1, planes - 1))
    landed, outer = lax.optimization_barrier((landed, outer))
    landed = landed.reshape(plane, tok_rows + pack, -1)
    doc_plane = landed[:, tok_rows, :tok_rows].reshape(-1)
    w_mine = landed[:, :tok_rows].reshape(plane * tok_rows, -1)
    w_all = lax.all_gather(w_mine, "z", axis=0, tiled=True)

    plane_rows = tok_rows * plane
    positions = first_pos + jnp.arange(plane_rows, dtype=jnp.int32)

    wo_late, w_all = lax.optimization_barrier((wo, w_all))
    inner = permuted(wo_late, "z", ahead, range(2, planes - 1))
    kv_acc = jnp.dot(normed_all, w_all[:, width:], preferred_element_type=jnp.float32)
    keys = rope(kv_acc[:, None, :HEAD_WIDTH], positions)[:, 0]
    kv_mine = jnp.concatenate([keys, kv_acc[:, HEAD_WIDTH:]], axis=1).astype(jnp.bfloat16)
    doc_fold = doc_plane.reshape(-1, 2 * HEAD_WIDTH)
    doc_fold = jnp.pad(doc_fold, ((0, -doc_fold.shape[0] % pack), (0, 0)))
    kv_docs = lax.all_gather(jnp.concatenate([kv_mine, doc_fold], axis=0), "z", axis=0)
    kv_all = kv_docs[:, :plane_rows].reshape(planes * plane_rows, -1)
    doc_all = kv_docs[:, plane_rows:].reshape(planes, -1)[:, :plane_rows].reshape(-1)
    doc_mine = doc_plane
    starts = jnp.sum((doc_all[None, :] < doc_mine[:, None]).astype(jnp.int32), axis=1)

    query_acc = jnp.dot(normed_all, w_all[:, :width], preferred_element_type=jnp.float32)
    queries = rope(query_acc.reshape(plane_rows, -1, HEAD_WIDTH), positions)
    queries = queries.astype(jnp.bfloat16).reshape(plane_rows, -1)

    inner, kv_all, starts, queries = lax.optimization_barrier((inner, kv_all, starts, queries))
    moved = [outer[0]] + inner + [outer[1]]
    half = plane_rows // 2
    block_rows = math.gcd(half, 256)
    lower = attend(queries[:half], kv_all, starts[:half], first_pos, block_rows, 512)
    lower, upper_queries = lax.optimization_barrier((lower, queries[half:]))
    lower_all = lax.all_gather(lower, "h", axis=1, tiled=True)
    upper = attend(upper_queries, kv_all, starts[half:], first_pos + half, block_rows, 512)
    upper_all = lax.all_gather(upper, "h", axis=1, tiled=True)
    level = lax.axis_index("z")
    wo_all = laid([wo] + moved, [(level - k) % planes for k in range(planes)], 1)
    lower_terms = jnp.dot(lower_all, wo_all, preferred_element_type=jnp.float32)
    upper_terms = jnp.dot(upper_all, wo_all, preferred_element_type=jnp.float32)
    terms = jnp.concatenate([lower_terms, upper_terms], axis=0).astype(jnp.bfloat16)
    rows_mine = lax.all_to_all(terms, "h", 0, 1, tiled=True)
    summed = rows_mine.reshape(tok_rows, plane, planes, -1).transpose(0, 2, 1, 3)
    summed = summed.reshape(tok_rows, model_width).astype(jnp.float32)
    return (source + summed).astype(jnp.bfloat16)


def plane_solution(mesh, planes):
    folded = jax.sharding.Mesh(mesh.devices.reshape(planes, KV_HEAD_COUNT), ("z", "h"))
    rows = P(("z", "h"))
    return jax.shard_map(
        plane_local,
        mesh=folded,
        in_specs=(rows, P(), rows, rows, rows, P(None, ("z", "h")), rows),
        out_specs=rows,
        check_vma=False,
    )


def solution(mesh):
    if mesh.shape["grp"] == 1 and mesh.shape["head"] == 1 and mesh.size == 4 * KV_HEAD_COUNT:
        return plane_solution(mesh, mesh.size // KV_HEAD_COUNT)
    in_specs = (
        P(("grp", "seq", "srv"), "head"),
        P(),
        P(("seq", "srv"), "head"),
        P(("seq", "srv"), "head"),
        P(("seq", "srv"), "head"),
        P("head", ("seq", "srv")),
        P(("grp", "seq", "srv")),
    )
    out_specs = P(("grp", "seq", "srv"), "head")
    return jax.shard_map(local, mesh=mesh, in_specs=in_specs, out_specs=out_specs, check_vma=False)
```
